32 devices in a mesh: parts: 2 (over x), lon: 16 (over z, y, core).
Axes of the slice: x: 2, y: 2, z: 4, core: 2. Of those that a mesh axis runs over, the one named last changes fastest.
Arguments:
- state: bfloat16 [128, 256, 512], P('parts', 'lon'), parts along dimension 0, may hold values from -6 to 6
- zonal_width: int32 [64], replicated, may hold values from 1 to 32, as said below
- tap_rows: int32 [64, 3], replicated, may hold values from 0 to 63, as said below
- filters: bfloat16 [2, 8, 64, 3, 65], replicated, may hold values from -0.875 to 0.875
- basis_mix: float32 [2, 8, 512], replicated, may hold values from -2 to 2
- norm_gain: float32 [2, 512], replicated, may hold values from 0.1 to 1.9
- weight_in: bfloat16 [2, 512, 1024], replicated, may hold values from -0.25 to 0.25
- bias_in: float32 [2, 1024], replicated, may hold values from -3 to 3
- weight_out: bfloat16 [2, 1024, 512], replicated, may hold values from -0.1875 to 0.1875
Outputs:
- advanced: bfloat16 [128, 256, 512], P('parts', 'lon'), parts along dimension 0
The draws below stay inside these ranges and needn't reach their ends.
There are 2 independent parts, one for each index of `parts`. The reference program is written for one: setup_inputs(seed, part) draws one part's arguments, and reference() takes and returns one part's arrays. A program takes and returns all parts, laid end to end along the dimension named above; an argument that names none is the same for every part. Nothing has to cross between parts.
Inputs may be any that keep to these rules, and one draw needn't show every extreme that they name: `zonal_width`: rows i with 16 <= i < 48 have widths of at most 16, and one of them has exactly 16; the first and last rows have 32. `tap_rows`: each entry differs from its own row index by at most 2.
All inputs are finite; a program needn't handle non-finite values.
Results may differ from the reference program's by a relative error of at most 0.0059.
Values may be sent and summed in bfloat16 or wider, within the bound.
A program may use at most 64 MiB of HBM per device.

```python
import jax
import jax.numpy as jnp
from jax import lax

C = 512
H = 1024
K = 8
TAPS = 3
HDEV = 2
L = 2
LAT = 64
LON_DEV = 16
MAXW = 32
LON = 256


def draw_zonal_width(key, part):
    row_ids = jnp.arange(LAT)
    quarter = LAT // 4
    polar_mask = (row_ids < quarter) | (row_ids >= LAT - quarter)
    first_key, second_key = jax.random.split(key)
    wide_width = jax.random.randint(first_key, (LAT,), LON_DEV, HDEV * LON_DEV + 1)
    narrow_width = jax.random.randint(second_key, (LAT,), 1, LON_DEV + 1)
    width = jnp.where(polar_mask, wide_width, narrow_width)
    width = jnp.where((row_ids == 0) | (row_ids == LAT - 1), HDEV * LON_DEV, width)
    width = jnp.where(row_ids == LAT // 2, LON_DEV, width)
    return width.astype(jnp.int32)


def draw_tap_rows(key, part):
    row_ids = jnp.arange(LAT)[:, None]
    centred = jnp.arange(TAPS)[None, :] - TAPS // 2
    jitter = jax.random.randint(jax.random.fold_in(key, 7), (LAT, TAPS), -1, 2)
    return jnp.clip(row_ids + centred + jitter, 0, LAT - 1).astype(jnp.int32)


def shard_levels(rng, dims, pieces, low, high):
    def one(axis_at, parts):
        steps = jax.random.uniform(jax.random.fold_in(jax.random.fold_in(rng, 6), axis_at), (parts,), jnp.float32, low / len(pieces), high / len(pieces))
        return jnp.repeat(jnp.exp(steps), dims[axis_at] // parts).reshape((-1,) + (1,) * (len(dims) - axis_at - 1))

    loudness = one(*pieces[0])
    for cut in pieces[1:]:
        loudness = loudness * one(*cut)
    return loudness


def noise(own_key, dims, spread, bound, shards=(), kind=jnp.bfloat16):
    level = shard_levels(own_key, dims, shards, -0.22, 0.18) if shards else 1.0
    array = jax.random.normal(own_key, dims, jnp.float32) * spread * level
    return jnp.minimum(jnp.maximum(array, -bound), bound).astype(kind)


def setup_inputs(seed: int = 0, part: int = 0) -> dict:
    keys = jax.random.split(jax.random.key(seed), 10)
    part_keys = jax.random.split(jax.random.fold_in(keys[9], part), 10)
    state = noise(part_keys[0], (LAT, LON, C), 1.0, 6.0, ((1, 16),))
    zonal_width = draw_zonal_width(jax.random.fold_in(keys[9], 71), part)
    tap_rows = draw_tap_rows(jax.random.fold_in(keys[9], 71), part)
    filters = noise(keys[3], (L, K, LAT, TAPS, 2 * MAXW + 1), (TAPS * LON_DEV) ** -0.5, 0.875)
    basis_mix = noise(keys[4], (L, K, C), K ** -0.5, 2.0, (), jnp.float32)
    norm_gain = jnp.clip(1.0 + 0.18 * jax.random.normal(keys[5], (L, C), jnp.float32), 0.1, 1.9)
    weight_in = noise(keys[6], (L, C, H), C ** -0.5, 0.25)
    bias_in = noise(keys[7], (L, H), 0.5, 3.0, (), jnp.float32)
    weight_out = noise(keys[8], (L, H, C), H ** -0.5, 0.1875)
    return {"state": state, "zonal_width": zonal_width, "tap_rows": tap_rows, "filters": filters, "basis_mix": basis_mix, "norm_gain": norm_gain, "weight_in": weight_in, "bias_in": bias_in, "weight_out": weight_out}


def layer_norm(filtered, gain):
    row_mean = lax.optimization_barrier(jnp.mean(filtered, axis=-1, keepdims=True))
    centred = filtered - row_mean
    row_var = lax.optimization_barrier(jnp.mean(centred * centred, axis=-1, keepdims=True))
    return (centred / jnp.sqrt(row_var + 1e-05) * gain).astype(jnp.bfloat16)

def disco_rows(field, tap_rows, filter_set, mix_set, zonal_width):
    lat_rows, lon_cells, channels = field.shape
    half_span = (filter_set.shape[-1] - 1) // 2
    widened = jnp.concatenate([field[:, lon_cells - half_span:], field, field[:, :half_span]], axis=1)
    offsets = jnp.arange(2 * half_span + 1, dtype=jnp.int32) - half_span
    in_support = jnp.abs(offsets)[None, :] <= zonal_width[:, None]
    masked = jnp.where(in_support[None, :, None, :], filter_set.astype(jnp.float32), jnp.float32(0))
    combined = jnp.einsum('kitd,kc->itdc', masked, mix_set.astype(jnp.float32), precision=lax.Precision.HIGHEST)

    def one_row(row_id):
        picked = jnp.take(widened, tap_rows[row_id], axis=0).astype(jnp.float32)
        row_weights = combined[row_id]

        def add_offset(offset, running):
            window = lax.dynamic_slice_in_dim(picked, offset, lon_cells, axis=1)
            tap_weight = lax.dynamic_index_in_dim(row_weights, offset, axis=1, keepdims=False)
            return running + lax.optimization_barrier(jnp.sum(tap_weight[:, None, :] * window, axis=0))
        return lax.fori_loop(0, 2 * half_span + 1, add_offset, jnp.zeros((lon_cells, channels), jnp.float32))
    return lax.map(one_row, jnp.arange(lat_rows, dtype=jnp.int32))

def reference(state, zonal_width, tap_rows, filters, basis_mix, norm_gain, weight_in, bias_in, weight_out):
    lat_rows, lon_cells, channels = state.shape
    current = state
    for layer_index in range(L):
        filtered = disco_rows(current, tap_rows, filters[layer_index], basis_mix[layer_index], zonal_width)
        normed = layer_norm(filtered, norm_gain[layer_index])
        flat_rows = normed.reshape(lat_rows * lon_cells, channels)
        pre_act = jnp.dot(flat_rows, weight_in[layer_index], preferred_element_type=jnp.float32) + bias_in[layer_index]
        hidden = jax.nn.gelu(pre_act, approximate=True).astype(jnp.bfloat16)
        update = jnp.dot(hidden, weight_out[layer_index], preferred_element_type=jnp.float32)
        current = (current.astype(jnp.float32) + update.reshape(lat_rows, lon_cells, channels)).astype(jnp.bfloat16)
    return current
```

```python
import functools

import jax
import jax.numpy as jnp
import numpy as np
from jax import lax
from jax.experimental import pallas as pl
from jax.experimental.pallas import tpu as pltpu
from jax.sharding import PartitionSpec as P

TILE = 256


def block_kernel(
    far, idx_ref, band_ref, *refs
):
    if far:
        (self_ref, outer_ref, inner_ref, outer_far_ref, inner_far_ref), refs = refs[:5], refs[5:]
    else:
        (self_ref, outer_ref, inner_ref), refs = refs[:3], refs[3:]
    mix_ref, gain_ref, win_ref, bin_ref, wout_ref, out_ref, filtered, held = refs
    rows, cells, channels = out_ref.shape
    first = pl.program_id(0) * rows
    basis = mix_ref.shape[0]
    depth = (15 if far else 9) * cells

    def one_row(i, carry):
        at = (first + i) * 12
        pieces = []
        taps = [[idx_ref[at + 3 * kind + t] for t in range(3)] for kind in range(3)]
        for ref in (outer_ref, self_ref, inner_ref):
            kind = 0 if ref is self_ref else 1
            pieces += [ref[taps[kind][t]] for t in range(3)]
        if far:
            for ref in (outer_far_ref, inner_far_ref):
                pieces += [ref[taps[2][t]] for t in range(3)]
        picked = jnp.concatenate(pieces, axis=0)
        terms = jnp.dot(band_ref[i, :, :depth], picked, preferred_element_type=jnp.float32)
        total = terms[:cells] * mix_ref[0:1, :]
        for k in range(1, basis):
            total = total + terms[k * cells:(k + 1) * cells] * mix_ref[k:k + 1, :]
        place = pl.ds(pl.multiple_of(i * cells, cells), cells)
        filtered[place, :] = total
        held[place, :] = self_ref[idx_ref[at + 9]]
        return carry

    lax.fori_loop(0, rows, one_row, 0, unroll=2)
    value = filtered[...]
    centred = value - jnp.mean(value, axis=-1, keepdims=True)
    var = jnp.mean(centred * centred, axis=-1, keepdims=True)
    normed = (centred * lax.rsqrt(var + 1e-05) * gain_ref[...]).astype(jnp.bfloat16)
    pre = jnp.dot(normed, win_ref[...], preferred_element_type=jnp.float32) + bin_ref[...]
    hidden = jax.nn.gelu(pre, approximate=True).astype(jnp.bfloat16)
    update = jnp.dot(hidden, wout_ref[...], preferred_element_type=jnp.float32)
    out = (held[...].astype(jnp.float32) + update).astype(jnp.bfloat16)
    out_ref[...] = out.reshape(rows, cells, channels)


def run_block(idx, band, fields, weights, far, blocks):
    mix, gain, win, bias, wout = weights
    total_rows = band.shape[0]
    rows = total_rows // blocks
    cells, channels = fields[0].shape[1:]
    whole = lambda a: pl.BlockSpec(a.shape, lambda g, s, n=a.ndim: (0,) * n)
    tail = list(fields) + [mix, gain, win, bias, wout]
    grid = pltpu.PrefetchScalarGridSpec(
        num_scalar_prefetch=1,
        grid=(blocks,),
        in_specs=[pl.BlockSpec((rows,) + band.shape[1:], lambda g, s: (g, 0, 0))]
        + [whole(a) for a in tail],
        out_specs=pl.BlockSpec((rows, cells, channels), lambda g, s: (g, 0, 0)),
        scratch_shapes=[
            pltpu.VMEM((rows * cells, channels), jnp.float32),
            pltpu.VMEM((rows * cells, channels), jnp.bfloat16),
        ],
    )
    flops = total_rows * cells * channels * (2 * 8 * 240 + 4 * win.shape[1])
    return pl.pallas_call(
        functools.partial(block_kernel, far),
        out_shape=jax.ShapeDtypeStruct((total_rows, cells, channels), jnp.bfloat16),
        grid_spec=grid,
        cost_estimate=pl.CostEstimate(
            flops=flops, bytes_accessed=16 * 2**20, transcendentals=total_rows * cells * 1024
        ),
        compiler_params=pltpu.CompilerParams(vmem_limit_bytes=44 * 2**20),
    )(idx, band, *tail)


def banded(filter_set, zonal_width, cells, sign):
    basis, lat, taps, offsets = filter_set.shape
    half = (offsets - 1) // 2
    d = jnp.arange(offsets, dtype=jnp.int32)
    support = jnp.abs(d - half)[None, :] <= zonal_width[:, None]
    masked = jnp.where(support[None, :, None, :], filter_set, jnp.zeros((), filter_set.dtype))
    masked = masked.transpose(1, 0, 2, 3).reshape(lat * basis, taps * offsets)
    col = jnp.arange(TILE, dtype=jnp.int32)
    piece, tap, m = col // (taps * cells), (col // cells) % taps, col % cells
    place = jnp.array([-1, 0, 1, -2, 2, 99], jnp.int32)[jnp.minimum(piece, 5)] * sign
    j = jnp.arange(cells, dtype=jnp.int32)
    want = place[None, :] * cells + m[None, :] - j[:, None] + half
    table = (
        (want[None, None] == d[None, :, None, None])
        & (tap[None, None, None, :] == jnp.arange(taps)[:, None, None, None])
    )
    table = table.astype(jnp.bfloat16).reshape(taps * offsets, cells * TILE)
    band = jnp.dot(masked, table, preferred_element_type=jnp.float32).astype(jnp.bfloat16)
    return band.reshape(lat, basis * cells, TILE)


def packed(rows, top, bottom, lat):
    return jnp.where(
        rows < top, rows, jnp.where(rows >= bottom, rows - bottom + top, rows + lat - bottom)
    )


def per_device(
    state, zonal_width, tap_rows, filters, basis_mix, norm_gain, weight_in, bias_in, weight_out
):
    lat, cells, channels = state.shape
    devices = lax.axis_size("lon")
    me = lax.axis_index("lon")
    sign = 1 - 2 * (me % 2)
    n = devices
    to_outer = [(i, (i - 1) % n if i % 2 == 0 else (i + 1) % n) for i in range(n)]
    to_inner = [(i, i ^ 1) for i in range(n)]
    to_far = [(i, (i + 2) % n if i % 2 == 0 else (i - 2) % n) for i in range(n)]
    send = lambda x, route: lax.ppermute(x, "lon", route)
    q = lat // 4
    ends = lambda x, a: jnp.concatenate([x[:a], x[lat - a:]], axis=0)

    def indices(rows, self_at, near_at, far_top):
        taps = tap_rows[rows]
        far_at = packed(taps, far_top, lat - far_top, lat)
        far_at = jnp.clip(far_at, 0, 2 * far_top - 1)
        own = self_at(jnp.asarray(rows, jnp.int32))[:, None]
        pad = jnp.zeros((len(rows), 2), jnp.int32)
        return jnp.concatenate([self_at(taps), near_at(taps), far_at, own, pad], axis=1).reshape(-1)

    def weights(l):
        return (
            basis_mix[l], norm_gain[l][None], weight_in[l], bias_in[l][None], weight_out[l]
        )


    same = lambda r: r
    a, b = q + 4, q + 2
    at_a = lambda r: packed(r, a, lat - a, lat)
    at_b = lambda r: packed(r, b, lat - b, lat)

    rows_p = np.concatenate([np.arange(b), np.arange(lat - b, lat)])
    rows_m = np.arange(b, lat - b)
    outer_p = send(ends(state, a), to_outer)
    far_out = send(ends(state, b), to_far)
    inner = send(jnp.concatenate([state[:a], state[lat - a:], state[a:lat - a]], axis=0), to_inner)
    late, outer_p = lax.optimization_barrier((state[a:lat - a], outer_p))
    far_in = send(jnp.concatenate([outer_p[:b], outer_p[2 * a - b:]], axis=0), to_inner)
    outer_m = send(late, to_outer)
    band1 = banded(filters[0], zonal_width, cells, sign)
    band2 = banded(filters[1], zonal_width, cells, sign)
    new_p = run_block(
        indices(rows_p, same, at_a, b), jnp.concatenate([band1[:b], band1[lat - b:]]),
        (state, outer_p, inner, far_out, far_in), weights(0), True, 2,
    )
    outer2_p = send(new_p, to_outer)
    far2_out = send(new_p, to_far)
    inner2_p = send(new_p, to_inner)
    new_m = run_block(
        indices(rows_m, same, at_a, b), band1[b:lat - b],
        (state, jnp.concatenate([outer_p, outer_m], axis=0), inner), weights(0), False, 2,
    )
    far2_in = send(outer2_p, to_inner)
    late2, outer2_p = lax.optimization_barrier((new_m, outer2_p))
    outer2_m = send(late2, to_outer)
    inner2_m = send(new_m, to_inner)
    rows_p2 = np.concatenate([np.arange(q), np.arange(lat - q, lat)])
    rows_m2 = np.arange(q, lat - q)
    out_p = run_block(
        indices(rows_p2, at_b, at_b, b), jnp.concatenate([band2[:q], band2[lat - q:]]),
        (new_p, outer2_p, inner2_p, far2_out, far2_in), weights(1), True, 2,
    )
    out_m = run_block(
        indices(rows_m2, at_b, at_b, b), band2[q:lat - q],
        (
            jnp.concatenate([new_p, new_m], axis=0),
            jnp.concatenate([outer2_p, outer2_m], axis=0),
            jnp.concatenate([inner2_p, inner2_m], axis=0),
        ), weights(1), False, 2,
    )
    return jnp.concatenate([out_p[:q], out_m, out_p[q:]], axis=0)


def solution(mesh):
    placed = (P("parts", "lon", None), P(), P(), P(), P(), P(), P(), P(), P())
    return jax.shard_map(
        per_device, mesh=mesh, in_specs=placed, out_specs=P("parts", "lon", None), check_vma=False
    )
```

```python
import functools

import jax
import jax.numpy as jnp
import numpy as np
from jax import lax
from jax.experimental import pallas as pl
from jax.experimental.pallas import tpu as pltpu
from jax.sharding import PartitionSpec as P

TILE = 256


def block_kernel(layer, far, parts, aliased, idx_ref, band_ref, *refs):
    fields = []
    for count in parts:
        fields.append(refs[:count])
        refs = refs[count:]
    mix_ref, gain_ref, win_ref, bin_ref, wout_ref = refs[:5]
    refs = refs[5 + aliased:]
    out_ref, filtered, held = refs[:3]
    joined = list(refs[3:])

    whole = []
    for pieces in fields:
        if len(pieces) == 1:
            whole.append(pieces[0])
            continue
        target = joined.pop(0)

        @pl.when(pl.program_id(0) == 0)
        def _(pieces=pieces, target=target):
            at = 0
            for piece in pieces:
                target[at:at + piece.shape[0]] = piece[...]
                at += piece.shape[0]

        whole.append(target)
    self_ref, outer_ref, inner_ref = whole[:3]
    rows, cells, channels = out_ref.shape
    first = pl.program_id(0) * rows
    basis = mix_ref.shape[0]
    depth = (15 if far else 9) * cells
    order = [(outer_ref, 1), (self_ref, 0), (inner_ref, 2)]
    if far:
        order += [(whole[3], 3), (whole[4], 3)]

    def one_row(i, carry):
        at = (first + i) * 16
        pieces = [ref[idx_ref[at + 3 * kind + t]] for ref, kind in order for t in range(3)]
        picked = jnp.concatenate(pieces, axis=0)
        terms = jnp.dot(band_ref[i, :, :depth], picked, preferred_element_type=jnp.float32)
        total = terms[:cells] * mix_ref[0:1, :]
        for k in range(1, basis):
            total = total + terms[k * cells:(k + 1) * cells] * mix_ref[k:k + 1, :]
        place = pl.ds(pl.multiple_of(i * cells, cells), cells)
        filtered[place, :] = total
        held[place, :] = self_ref[idx_ref[at + 12]]
        return carry

    lax.fori_loop(0, rows, one_row, 0, unroll=2)
    value = filtered[...]
    centred = value - jnp.mean(value, axis=-1, keepdims=True)
    var = jnp.mean(centred * centred, axis=-1, keepdims=True)
    gain = gain_ref[layer:layer + 1, :]
    normed = (centred * lax.rsqrt(var + 1e-05) * gain).astype(jnp.bfloat16)
    pre = jnp.dot(normed, win_ref[...], preferred_element_type=jnp.float32)
    pre = pre + bin_ref[layer:layer + 1, :]
    hidden = jax.nn.gelu(pre, approximate=True).astype(jnp.bfloat16)
    update = jnp.dot(hidden, wout_ref[...], preferred_element_type=jnp.float32)
    out = (held[...].astype(jnp.float32) + update).astype(jnp.bfloat16)
    out_ref[...] = out.reshape(rows, cells, channels)


def run_block(layer, idx, band, starts, rows, fields, weights, into=None, out_rows=None):
    mix, gain, win, bias, wout = weights
    base, step = starts[0], starts[1] - starts[0]
    far = len(fields) == 5
    cells, channels = fields[0][0].shape[1:]
    whole = lambda a: pl.BlockSpec(a.shape, lambda g, s, n=a.ndim: (0,) * n)
    one = lambda a: pl.BlockSpec((None,) + a.shape[1:], lambda g, s: (layer, 0, 0))
    flat = [a for f in fields for a in f]
    tail = flat + [mix, gain, win, bias, wout]
    in_specs = [
        pl.BlockSpec(
            (pl.Element(rows), pl.Element(band.shape[1]), pl.Element(band.shape[2])),
            lambda g, s: (base + g * step, 0, 0),
        )
    ]
    in_specs += [whole(a) for a in flat]
    in_specs += [one(mix), whole(gain), one(win), whole(bias), one(wout)]
    if into is not None:
        tail.append(into)
        in_specs.append(pl.BlockSpec(memory_space=pl.ANY))
    if out_rows is None:
        out_rows, place = 2 * rows, lambda g, s: (g, 0, 0)
    else:
        place = lambda g, s: (base // rows + g * (step // rows), 0, 0)
    joined = [
        pltpu.VMEM((sum(a.shape[0] for a in f), cells, channels), jnp.bfloat16)
        for f in fields if len(f) > 1
    ]
    grid = pltpu.PrefetchScalarGridSpec(
        num_scalar_prefetch=1,
        grid=(2,),
        in_specs=in_specs,
        out_specs=pl.BlockSpec((rows, cells, channels), place),
        scratch_shapes=[
            pltpu.VMEM((rows * cells, channels), jnp.float32),
            pltpu.VMEM((rows * cells, channels), jnp.bfloat16),
        ] + joined,
    )
    flops = 2 * rows * cells * channels * (2 * 8 * 240 + 4 * win.shape[2])
    return pl.pallas_call(
        functools.partial(
            block_kernel, layer, far, tuple(len(f) for f in fields), 0 if into is None else 1
        ),
        out_shape=jax.ShapeDtypeStruct((out_rows, cells, channels), jnp.bfloat16),
        grid_spec=grid,
        input_output_aliases={} if into is None else {1 + len(tail): 0},
        cost_estimate=pl.CostEstimate(
            flops=flops, bytes_accessed=16 * 2**20, transcendentals=2 * rows * cells * 1024
        ),
        compiler_params=pltpu.CompilerParams(vmem_limit_bytes=44 * 2**20),
    )(idx, band, *tail)


def banded(filter_set, zonal_width, cells, sign):
    basis, lat, taps, offsets = filter_set.shape
    half = (offsets - 1) // 2
    d = jnp.arange(offsets, dtype=jnp.int32)
    support = jnp.abs(d - half)[None, :] <= zonal_width[:, None]
    masked = jnp.where(support[None, :, None, :], filter_set, jnp.zeros((), filter_set.dtype))
    masked = masked.transpose(1, 0, 2, 3).reshape(lat * basis, taps * offsets)
    col = jnp.arange(TILE, dtype=jnp.int32)
    piece, tap, m = col // (taps * cells), (col // cells) % taps, col % cells
    place = jnp.array([-1, 0, 1, -2, 2, 99], jnp.int32)[jnp.minimum(piece, 5)] * sign
    j = jnp.arange(cells, dtype=jnp.int32)
    want = place[None, :] * cells + m[None, :] - j[:, None] + half
    table = (
        (want[None, None] == d[None, :, None, None])
        & (tap[None, None, None, :] == jnp.arange(taps)[:, None, None, None])
    )
    table = table.astype(jnp.bfloat16).reshape(taps * offsets, cells * TILE)
    band = jnp.dot(masked, table, preferred_element_type=jnp.float32).astype(jnp.bfloat16)
    return band.reshape(lat, basis * cells, TILE)


def packed(rows, top, bottom, lat):
    return jnp.where(
        rows < top, rows, jnp.where(rows >= bottom, rows - bottom + top, rows + lat - bottom)
    )


def per_device(
    state, zonal_width, tap_rows, filters, basis_mix, norm_gain, weight_in, bias_in, weight_out
):
    lat, cells, channels = state.shape
    devices = lax.axis_size("lon")
    me = lax.axis_index("lon")
    sign = 1 - 2 * (me % 2)
    n = devices
    to_outer = [(i, (i - 1) % n if i % 2 == 0 else (i + 1) % n) for i in range(n)]
    to_inner = [(i, i ^ 1) for i in range(n)]
    to_far = [(i, (i + 2) % n if i % 2 == 0 else (i - 2) % n) for i in range(n)]
    send = lambda x, route: lax.ppermute(x, "lon", route)
    q = lat // 4
    ends = lambda x, a: jnp.concatenate([x[:a], x[lat - a:]], axis=0)

    def indices(rows, self_at, outer_at, inner_at, far_top):
        taps = jnp.concatenate([tap_rows[lo:hi] for lo, hi in rows], axis=0)
        own = jnp.asarray(np.concatenate([np.arange(lo, hi) for lo, hi in rows]), jnp.int32)
        far_at = packed(taps, far_top, lat - far_top, lat)
        far_at = jnp.clip(far_at, 0, 2 * far_top - 1)
        own = self_at(own)[:, None]
        pad = jnp.zeros((taps.shape[0], 3), jnp.int32)
        cols = [self_at(taps), outer_at(taps), inner_at(taps), far_at, own, pad]
        return jnp.concatenate(cols, axis=1).reshape(-1)

    weights = (basis_mix, norm_gain, weight_in, bias_in, weight_out)
    same = lambda r: r
    a, b = q + 4, q + 2
    at_a = lambda r: packed(r, a, lat - a, lat)
    at_b = lambda r: packed(r, b, lat - b, lat)
    mid_a, mid_q = (lat - 2 * b) // 2, (lat - 2 * q) // 2

    outer_p = send(ends(state, a), to_outer)
    far_out = send(ends(state, b), to_far)
    inner = send(state, to_inner)
    late, outer_p = lax.optimization_barrier((state[a:lat - a], outer_p))
    far_in = send(jnp.concatenate([outer_p[:b], outer_p[2 * a - b:]], axis=0), to_inner)
    outer_m = send(late, to_outer)
    band1, band2, idx1p, idx1m, idx2p, idx2m = lax.optimization_barrier((
        banded(filters[0], zonal_width, cells, sign),
        banded(filters[1], zonal_width, cells, sign),
        indices([(0, b), (lat - b, lat)], same, at_a, same, b),
        indices([(b, lat - b)], same, at_a, same, b),
        indices([(0, q), (lat - q, lat)], at_b, at_b, at_b, b),
        indices([(q, lat - q)], at_b, at_b, at_b, b),
    ))
    new_p = run_block(
        0, idx1p, band1, (0, lat - b), b,
        ((state,), (outer_p,), (inner,), (far_out,), (far_in,)), weights,
    )
    outer2_p = send(new_p, to_outer)
    far2_out = send(new_p, to_far)
    inner2_p = send(new_p, to_inner)
    new_m = run_block(
        0, idx1m, band1, (b, b + mid_a), mid_a,
        ((state,), (outer_p, outer_m), (inner,)), weights,
    )
    late2, outer2_p = lax.optimization_barrier((new_m, outer2_p))
    far2_in = send(outer2_p, to_inner)
    outer2_m = send(late2, to_outer)
    inner2_m = send(new_m, to_inner)
    out = run_block(
        1, idx2p, band2, (0, lat - q), q,
        ((new_p,), (outer2_p,), (inner2_p,), (far2_out,), (far2_in,)), weights, out_rows=lat,
    )
    return run_block(
        1, idx2m, band2, (q, q + mid_q), mid_q,
        ((new_p, new_m), (outer2_p, outer2_m), (inner2_p, inner2_m)), weights,
        into=out, out_rows=lat,
    )


def solution(mesh):
    placed = (P("parts", "lon", None), P(), P(), P(), P(), P(), P(), P(), P())
    return jax.shard_map(
        per_device, mesh=mesh, in_specs=placed, out_specs=P("parts", "lon", None), check_vma=False
    )
```
